256 devices in a mesh: prow: 16 (over z, core), pcol: 16 (over x, y).
Axes of the slice: x: 4, y: 4, z: 8, core: 2. Of those that a mesh axis runs over, the one named last changes fastest.
Arguments:
- rhs: bfloat16 [4, 16, 1024, 128], P(None, 'prow', 'pcol'), may hold values from -6 to 6
- diag_inv: bfloat16 [4, 16, 1024, 1024], P(None, 'prow', 'pcol'), as said below
- panel: bfloat16 [3, 16, 28672, 1024], P(None, 'prow', 'pcol'), may hold values from -0.03125 to 0.03125
- owner: int32 [3, 16, 224, 1], P(None, 'prow', 'pcol'), may hold values from 0 to 15; in each aligned block of 14 rows (0 to 13, 14 to 27, ..., all dimensions but the last counted through in order) at most 2 rows name the same one
- target_block: int32 [3, 16, 224], P(None, 'prow', 'pcol'), may hold values from 0 to 7
- row_map: int32 [3, 16, 224, 128], P(None, 'prow', 'pcol'), may hold values from -1 to 127, as said below
Outputs:
- solution: bfloat16 [4, 16, 1024, 128], P(None, 'prow', 'pcol')
The draws below stay inside these ranges and needn't reach their ends.
Inputs may be any that keep to these rules, and one draw needn't show every extreme that they name: In each level, the 14 consecutive blocks of one supernode that one index of pcol holds name one owner at most 2 times. `row_map`: -1 marks a padded row. `diag_inv`: zero above the diagonal.
All inputs are finite; a program needn't handle non-finite values.
Results may differ from the reference program's by a relative error of at most 0.02.
Values may be sent and summed in bfloat16 or wider, within the bound.
A program may use at most 64 MiB of HBM per device.

```python
import math
import jax
import jax.numpy as jnp
import numpy as np
from jax import lax

W = 1024
BLOCK = 128
R = 128
LEVELS = 4
PB_DEV = 14
CAP = 2
SUPERNODES = 16
PB = 224


def draw_diag_inv(key, part):
    first, second = jax.random.split(key)
    shape = (LEVELS, SUPERNODES, W, W)
    below = jax.random.normal(first, shape, jnp.float32) / math.sqrt(W)
    leading = jax.random.uniform(second, (LEVELS, SUPERNODES, W, 1), jnp.float32, 0.6, 1.4)
    rows_i = lax.broadcasted_iota(jnp.int32, (W, W), 0)
    cols_i = lax.broadcasted_iota(jnp.int32, (W, W), 1)
    lower = jnp.where(rows_i > cols_i, below, 0.0)
    diagonal = jnp.where(rows_i == cols_i, 1.0, 0.0) * leading
    return (lower + diagonal).astype(jnp.bfloat16)


def draw_row_map(key, part):
    first, second = jax.random.split(key)
    shape = (LEVELS - 1, SUPERNODES, PB, BLOCK)
    picked = jax.random.randint(first, shape, 0, BLOCK)
    padding = jax.random.randint(second, shape, 0, 4)
    return jnp.where(padding == 0, -1, picked).astype(jnp.int32)


def set_ends(drawn, key, low, largest):
    shape = drawn.shape
    place = [jax.random.randint(jax.random.fold_in(key, axis), (), 0, shape[axis]) for axis in range(len(shape))]
    drawn = drawn.at[tuple(place)].set(low)
    longest = shape.index(max(shape))
    place[longest] = (place[longest] + 1) % shape[longest]
    return drawn.at[tuple(place)].set(largest)


def shard_levels(rng, dims, cuts, smallest, top_value):
    def one(dim, blocks):
        heights = jax.random.uniform(jax.random.fold_in(jax.random.fold_in(rng, 6), dim), (blocks,), jnp.float32, smallest / len(cuts), top_value / len(cuts))
        return jnp.repeat(jnp.exp(heights), dims[dim] // blocks).reshape((-1,) + (1,) * (len(dims) - dim - 1))

    level = one(*cuts[0])
    for cut in cuts[1:]:
        level = level * one(*cut)
    return level


def assign_block(rng, own, number, rows, count, top, limit, lean):
    ranking = jax.random.permutation(rng, count)
    heavy_load, common = load_shares(count, rows * top, limit, lean, True), load_shares(count, rows * top, limit, lean, False)
    places = jnp.arange(count)

    def named(tallies, offset_by):
        used = int((tallies > 0).sum())
        fixed = max(1, used // 4)
        moved = fixed + (places - fixed + offset_by * (used - fixed)) % max(1, count - fixed)
        return jnp.zeros((count,), jnp.int32).at[ranking[jnp.where(places < fixed, places, moved)]].set(jnp.asarray(tallies, jnp.int32))

    tallies = jnp.where(number % 4 == 0, named(heavy_load, number // 4), named(common, number - number // 4 - 1))
    mixed = jax.random.permutation(jax.random.fold_in(own, 3), count)
    source_of, taker = mixed[0:count // 2 * 2:2], mixed[1:count // 2 * 2:2]
    margin = jnp.minimum(tallies[source_of] - 1, limit - tallies[taker]) // 2
    margin = jnp.where((source_of == ranking[0]) | (taker == ranking[0]) | (tallies[taker] == 0), 0, jnp.maximum(margin, 0))
    moved = jax.random.randint(jax.random.fold_in(own, 4), (count // 2,), 0, 1 << 20) % (margin + 1)
    tallies = tallies.at[source_of].add(-moved).at[taker].add(moved)
    items = jnp.searchsorted(jnp.cumsum(tallies), jnp.arange(rows * top), side="right").astype(jnp.int32)
    listing = items.reshape(top, rows).T
    listing = listing[jax.random.permutation(jax.random.fold_in(own, 1), rows)]
    offset_by = jax.random.randint(jax.random.fold_in(own, 2), (rows, 1), 0, top)
    return jnp.take_along_axis(listing, (jnp.arange(top)[None, :] + offset_by) % top, axis=1)


def load_shares(count, total, most, lean, full):
    weights = [(1 << 20) // math.isqrt(grade ** lean) + 1 for grade in range(1, count + 1)]
    largest = most if full else min(most, max(-(-total // count), total * weights[0] // sum(weights)))
    least = 1 if total - largest >= count - 1 else 0
    holding, rest = [largest] + [least] * (count - 1), total - largest - least * (count - 1)
    while rest > 0:
        candidates = [i for i in range(1, count) if holding[i] < largest] or [i for i in range(1, count) if holding[i] < most]
        mass, remaining = sum([weights[i] for i in candidates]), rest
        for i in candidates:
            more = min(most - holding[i], max(1, remaining * weights[i] // mass), rest)
            holding[i] = holding[i] + more
            rest = rest - more
    return np.array(holding)


def noise(stream_key, extent, scale, most, pieces=(), held_as=jnp.bfloat16):
    values = jax.random.normal(stream_key, extent, jnp.float32) * scale
    if len(pieces) > 0:
        values = shard_levels(stream_key, extent, pieces, -0.22, 0.18) * values
    return jnp.clip(values, min=-most, max=most).astype(held_as)


def setup_inputs(seed: int = 0) -> dict:
    splits = jax.random.split(jax.random.key(seed), 7)
    rhs = noise(splits[0], (LEVELS, SUPERNODES, W, R), 1.0, 6.0, ((1, 16), (2, 16)))
    diag_inv = draw_diag_inv(jax.random.fold_in(splits[6], 71), 0)
    panel = noise(splits[2], (LEVELS - 1, SUPERNODES, PB * BLOCK, W), (PB * BLOCK) ** -0.5, 0.03125, ((1, 16), (2, 16)))
    owner_keys = jax.random.split(jax.random.fold_in(splits[3], 1), (LEVELS - 1) * SUPERNODES * PB // PB_DEV)
    owner_turns = jax.random.permutation(jax.random.fold_in(splits[3], 3), (LEVELS - 1) * SUPERNODES * PB // PB_DEV)
    owner = jax.vmap(lambda own, number: assign_block(jax.random.fold_in(splits[3], 2), own, number, PB_DEV, SUPERNODES, 1, CAP, 2))(owner_keys, owner_turns).reshape((LEVELS - 1, SUPERNODES, PB, 1))
    target_block = set_ends(jax.random.randint(splits[4], (LEVELS - 1, SUPERNODES, PB), 0, W // BLOCK), jax.random.fold_in(splits[4], 1), 0, (W // BLOCK) - 1).astype(jnp.int32)
    row_map = draw_row_map(jax.random.fold_in(splits[6], 71), 0)
    return {"rhs": rhs, "diag_inv": diag_inv, "panel": panel, "owner": owner, "target_block": target_block, "row_map": row_map}


def targets(owner_level, block_level, map_level):
    index = owner_level[:, :, 0][:, :, None] * W + block_level[:, :, None] * BLOCK + map_level
    valid = map_level >= 0
    index = jnp.where(valid, index, 0).astype(jnp.int32)
    return index.reshape(-1), valid.reshape(-1)


def forward_product(pair):
    return jnp.dot(pair[0], pair[1], preferred_element_type=jnp.float32).astype(jnp.bfloat16)


def transposed_product(pair):
    return lax.dot_general(pair[0], pair[1], (((0,), (0,)), ((), ())), preferred_element_type=jnp.float32)


def reference(rhs, diag_inv, panel, owner, target_block, row_map):
    supers = rhs.shape[1]
    solved = []
    carried = None
    for level in range(LEVELS):
        if level == 0:
            rights = rhs[0]
        else:
            rights = (rhs[level].astype(jnp.float32) - carried.reshape(supers, W, R)).astype(jnp.bfloat16)
        solved_level = lax.map(forward_product, (diag_inv[level], rights))
        solved.append(solved_level)
        if level < LEVELS - 1:
            update = lax.map(forward_product, (panel[level], solved_level))
            index, valid = targets(owner[level], target_block[level], row_map[level])
            rows_f = update.reshape(-1, R).astype(jnp.float32)
            carried = jnp.zeros((supers * W, R), jnp.float32).at[index].add(jnp.where(valid[:, None], rows_f, jnp.float32(0.0)))
    outputs = [None] * LEVELS
    parent_flat = None
    for level in reversed(range(LEVELS)):
        if level == LEVELS - 1:
            values = solved[level]
        else:
            index, valid = targets(owner[level], target_block[level], row_map[level])
            picked = jnp.take(parent_flat, index, axis=0)
            gathered = jnp.where(valid[:, None], picked, jnp.zeros_like(picked)).astype(jnp.bfloat16)
            gathered = gathered.reshape(supers, PB * BLOCK, R)
            back = lax.map(transposed_product, (panel[level], gathered))
            values = (solved[level].astype(jnp.float32) - back).astype(jnp.bfloat16)
        answer = lax.map(transposed_product, (diag_inv[level], values)).astype(jnp.bfloat16)
        outputs[level] = answer
        parent_flat = answer.reshape(supers * W, R)
    return jnp.stack(outputs)
```

```python
import functools

import jax
import jax.numpy as jnp
from jax import lax
from jax.experimental import pallas as pl
from jax.experimental.pallas import tpu as pltpu
from jax.sharding import PartitionSpec as P

MESH = pl.DeviceIdType.MESH
N = 16
F32 = jnp.float32
BF16 = jnp.bfloat16


def nt(a, b):
    return lax.dot_general(a, b, (((1,), (1,)), ((), ())), preferred_element_type=F32)


def nn(a, b):
    return jnp.dot(a, b, preferred_element_type=F32)


S_C0, S_Y0, S_V, S_R, S_F1, S_F2, S_F3, S_B1, S_B2, S_B3, S_OUT, S_X0 = (
    0, 1, 2, 3, 4, 7, 10, 13, 16, 19, 22, 25)
NSEM = 26


def kernel(rhs, dinv, panel_hbm, vcode, rmap, out,
           panel, dfull, emat, c0, y0, sr, rr, rhsc, vall, yt, ct,
           s1, r1, s2, r2, s3, r3, sb1, rb1, s4, r4, gt, tt, wt, s5, r5, so, ro, s7, r7, xf, tile,
           psem, ssem, rsem, dss, drs):
    p = lax.axis_index("prow")
    c = lax.axis_index("pcol")
    x, y = c // 4, c % 4

    def plane_dev(d):
        return (p, lax.rem(x + d // 4, 4) * 4 + lax.rem(y + d % 4, 4))

    def col_dev(d):
        return (lax.rem(p + d, N), c)

    for l in range(3):
        pltpu.make_async_copy(panel_hbm.at[l], panel.at[l], psem.at[l]).start()

    bar = pltpu.get_barrier_semaphore()

    def greet(d, _):
        pl.semaphore_signal(bar, inc=1, device_id=plane_dev(d), device_id_type=MESH)
        pl.semaphore_signal(bar, inc=1, device_id=col_dev(d), device_id_type=MESH)
        return 0

    c0[c] = rhs[0]
    vall[c] = vcode[...]
    r1[:, :, 112:128, :] = jnp.zeros((3, N, 16, 128), BF16)
    lax.fori_loop(1, N, greet, 0)
    pl.semaphore_wait(bar, 30)

    def spread(dev, src, dst, sem):
        def step(d, _):
            to = dev(d)
            pltpu.make_async_remote_copy(src(to), dst, ssem.at[sem], rsem.at[sem], device_id=to, device_id_type=MESH).start()
            return 0
        lax.fori_loop(1, N, step, 0)

    def wait_all(ref, sem):
        pltpu.make_async_copy(ref, ref, sem).wait()

    spread(plane_dev, lambda to: c0.at[c], c0.at[c], S_C0)
    spread(plane_dev, lambda to: vall.at[c], vall.at[c], S_V)
    for l in range(0, 4, 2):
        halves = []
        for k in (l, l + 1):
            r = rhs[k].astype(F32)
            halves.append(jnp.concatenate([r, r], axis=0).T.reshape(N, 8, 128))
        sr[:, l * 8:l * 8 + 16, :] = jnp.concatenate(halves, axis=1).astype(BF16)
    rr[c] = sr[c]
    spread(plane_dev, lambda to: sr.at[to[1]], rr.at[c], S_R)
    wait_all(c0.at[pl.ds(0, 15)], rsem.at[S_C0])
    y0[c] = nn(dinv[0], c0[...].reshape(1024, 128)).astype(BF16)
    spread(plane_dev, lambda to: y0.at[c], y0.at[c], S_Y0)

    wait_all(rr.at[pl.ds(0, 15)], rsem.at[S_R])
    first = lax.broadcasted_iota(jnp.int32, (8, 128), 1) < 64
    for l in range(1, 4):
        for tb in range(8):
            a = rr[2 * tb, :, :].astype(F32)[8 * l:8 * l + 8]
            b = rr[2 * tb + 1, :, :].astype(F32)[8 * l:8 * l + 8]
            rhsc[l, tb * 8:tb * 8 + 8, :] = jnp.where(first, a, b)
    wait_all(vall.at[pl.ds(0, 15)], rsem.at[S_V])

    def build_e(l):
        rows = lax.broadcasted_iota(jnp.int32, (1024, 128), 0)

        def one(s, _):
            v = vall[s, pl.ds(l, 1), :]
            emat[:, pl.ds(pl.multiple_of(s * 128, 128), 128)] = jnp.where(rows == v, 1.0, 0.0).astype(BF16)
            return 0
        lax.fori_loop(0, N, one, 0)

    def build_et(l, ematt):
        lanes = lax.broadcasted_iota(jnp.int32, (128, 1024), 1).astype(F32)

        def one(s, _):
            v = jnp.broadcast_to(vall[s, pl.ds(l, 1), :].astype(F32), (128, 128)).T
            v = jnp.concatenate([v] * 8, axis=1)
            ematt[pl.ds(pl.multiple_of(s * 128, 128), 128), :] = jnp.where(lanes == v, 1.0, 0.0).astype(BF16)
            return 0
        lax.fori_loop(0, N, one, 0)

    def d_tile(l, m, rows):
        return dfull.at[l, rows, pl.ds(m * 256, 256)]

    def start_d(l):
        mine = pl.ds(pl.multiple_of(c * 64, 64), 64)
        dfull[l, mine, :] = dinv[l]
        for m in range(4):
            @pl.when(c >= 4 * m)
            def _():
                def step(d, _):
                    pltpu.make_async_remote_copy(
                        dinv.at[l, :, pl.ds(m * 256, 256)], d_tile(l, m, mine), dss.at[l, m], drs.at[l, m],
                        device_id=plane_dev(d), device_id_type=MESH).start()
                    return 0
                lax.fori_loop(1, N, step, 0)

    def wait_d(l):
        for m in range(4):
            n = 16 - 4 * m

            @pl.when(c >= 4 * m)
            def _():
                wait_all(d_tile(l, m, pl.ds(0, 64 * (n - 1))), drs.at[l, m])

            @pl.when(c < 4 * m)
            def _():
                wait_all(d_tile(l, m, pl.ds(0, 64 * n)), drs.at[l, m])

    def place(l, b):
        rows = lax.broadcasted_iota(jnp.int32, (128, 128), 0)
        return jnp.where(rows == rmap[l, pl.ds(b, 1), :], 1.0, 0.0).astype(BF16)

    wait_all(y0.at[pl.ds(0, 15)], rsem.at[S_Y0])
    for i in range(8):
        yt[0, :, i * 128:i * 128 + 128] = y0[2 * i:2 * i + 2].reshape(128, 128).astype(F32).T.astype(BF16)

    def forward(l, _):
        pltpu.make_async_copy(panel_hbm.at[l], panel.at[l], psem.at[l]).wait()

        def pair(n, _):
            u = nt(yt[l], panel[l, pl.ds(pl.multiple_of(n * 256, 256), 256), :]).astype(BF16)
            a = nt(u[:, :128], place(l, 2 * n)).reshape(N, 8, 128)
            b = nt(u[:, 128:], place(l, 2 * n + 1)).reshape(N, 8, 128)
            s1[l, :, pl.ds(pl.multiple_of(n * 16, 16), 16), :] = jnp.concatenate([a, b], axis=1).astype(BF16)
            return 0
        lax.fori_loop(0, 7, pair, 0)
        r1[l, c, 0:112, :] = s1[l, c]
        spread(plane_dev, lambda to: s1.at[l, to[1]], r1.at[l, c, pl.ds(0, 112), :], S_F1 + l)
        build_e(l)
        start_d(l + 1)
        wait_all(r1.at[l, pl.ds(0, 15), pl.ds(0, 112), :], rsem.at[S_F1 + l])

        def owners(n, _):
            rows = nn(emat[pl.ds(pl.multiple_of(n * 256, 256), 256), :], r1[l].reshape(2048, 128))
            s2[l, pl.ds(n * 4, 4)] = rows.astype(BF16).reshape(4, 64, 128)
            return 0
        lax.fori_loop(0, 4, owners, 0)
        r2[l, p] = s2[l, p]
        spread(col_dev, lambda to: s2.at[l, to[0]], r2.at[l, p], S_F2 + l)
        wait_all(r2.at[l, pl.ds(0, 15)], rsem.at[S_F2 + l])
        carried = jnp.sum(r2[l].astype(F32), axis=0)
        s3[l] = (rhsc[l + 1] - carried).astype(BF16)
        r3[l, c] = s3[l]
        spread(plane_dev, lambda to: s3.at[l], r3.at[l, c], S_F3 + l)
        wait_all(r3.at[l, pl.ds(0, 15)], rsem.at[S_F3 + l])
        got = r3[l].astype(F32).reshape(N, 8, 8, 128)
        for tb in range(8):
            ct[:, tb * 128:tb * 128 + 128] = got[:, tb].reshape(128, 128).astype(BF16)
        wait_d(l + 1)
        for i in range(4):
            k = 256 * (i + 1)
            yt[l + 1, :, i * 256:k] = nt(ct[:, :k], dfull[l + 1, i * 256:k, :k]).astype(BF16)
        return 0

    lax.fori_loop(0, 3, forward, 0)

    def back_solve(l):
        for m in range(4):
            xf[:, m * 256:m * 256 + 256] = nn(wt[:, m * 256:], dfull[l, m * 256:, m * 256:m * 256 + 256])

    def my_rows(tile_value):
        tile[...] = tile_value.T
        return tile[pl.ds(pl.multiple_of(lax.rem(c, 2) * 64, 64), 64), :].astype(BF16)

    wt[...] = yt[3]
    back_solve(3)
    mine8 = pl.ds(pl.multiple_of(c * 8, 8), 8)
    for tb in range(0, 8, 2):
        sb1[2, tb * 8:tb * 8 + 16, :] = jnp.concatenate(
            [xf[mine8, tb * 128:tb * 128 + 128], xf[mine8, tb * 128 + 128:tb * 128 + 256]], axis=0).astype(BF16)
    my_tile = c // 2

    def backward_to_partials(l):
        rb1[l, p] = sb1[l]
        spread(col_dev, lambda to: sb1.at[l], rb1.at[l, p], S_B1 + l)
        build_et(l, ematt=emat_t)
        wait_all(rb1.at[l, pl.ds(0, 15)], rsem.at[S_B1 + l])

        def holders(n, _):
            rows = nn(emat_t[pl.ds(pl.multiple_of(n * 256, 256), 256), :], rb1[l].reshape(1024, 128))
            s4[l, pl.ds(n * 2, 2)] = rows.astype(BF16).reshape(2, 128, 128)
            return 0
        lax.fori_loop(0, 8, holders, 0)
        r4[l, c] = s4[l, c, 0:112, :]
        spread(plane_dev, lambda to: s4.at[l, to[1], pl.ds(0, 112), :], r4.at[l, c], S_B2 + l)

    def backward_rest(l):
        wait_all(r4.at[l, pl.ds(0, 15)], rsem.at[S_B2 + l])

        def pair(n, _):
            got = r4[l, :, pl.ds(pl.multiple_of(n * 16, 16), 16), :].astype(F32)
            a = nn(got[:, :8].reshape(128, 128).astype(BF16), place(l, 2 * n))
            b = nn(got[:, 8:].reshape(128, 128).astype(BF16), place(l, 2 * n + 1))
            gt[:, pl.ds(pl.multiple_of(n * 256, 256), 256)] = jnp.concatenate([a, b], axis=1).astype(BF16)
            return 0
        lax.fori_loop(0, 7, pair, 0)

        def columns(n, _):
            cols = pl.ds(pl.multiple_of(n * 256, 256), 256)
            t = nn(gt[...], panel[l, :, cols])
            wt[:, cols] = (yt[l, :, cols].astype(F32) * (1.0 / 16) - t).astype(BF16)
            return 0
        lax.fori_loop(0, 4, columns, 0)
        back_solve(l)

    emat_t = tt

    def backward(m, _):
        l = 2 - m
        backward_to_partials(l)

        @pl.when(m == 0)
        def _():
            start_d(0)
        backward_rest(l)
        for tb in range(0, 8, 2):
            a = xf[:, tb * 128:tb * 128 + 128].reshape(N, 8, 128)
            b = xf[:, tb * 128 + 128:tb * 128 + 256].reshape(N, 8, 128)
            s5[l, :, tb * 8:tb * 8 + 16, :] = jnp.concatenate([a, b], axis=1).astype(BF16)
        r5[l, c] = s5[l, c]
        spread(plane_dev, lambda to: s5.at[l, to[1]], r5.at[l, c], S_B3 + l)
        wait_all(r5.at[l, pl.ds(0, 15)], rsem.at[S_B3 + l])
        total = jnp.sum(r5[l].astype(F32), axis=0).astype(BF16)
        sb1[l - 1] = total
        so[l] = total.astype(F32).reshape(8, 8, 128)
        ro[l, c] = so[l, my_tile]
        spread(plane_dev, lambda to: so.at[l, to[1] // 2], ro.at[l, c], S_OUT + l)
        return 0

    out[3] = my_rows(xf[:, pl.ds(pl.multiple_of(my_tile * 128, 128), 128)])
    lax.fori_loop(0, 2, backward, 0)
    backward_to_partials(0)
    for l in (2, 1):
        wait_all(ro.at[l, pl.ds(0, 15)], rsem.at[S_OUT + l])
        out[l] = my_rows(ro[l].reshape(128, 128))
    wait_d(0)
    backward_rest(0)
    for i in range(8):
        s7[2 * i:2 * i + 2] = xf[:, i * 128:i * 128 + 128].T.astype(BF16).reshape(2, 64, 128)
    r7[c] = s7[c]
    spread(plane_dev, lambda to: s7.at[to[1]], r7.at[c], S_X0)
    wait_all(r7.at[pl.ds(0, 15)], rsem.at[S_X0])
    out[0] = jnp.sum(r7[...].astype(F32), axis=0).astype(BF16)

    wait_all(c0.at[pl.ds(0, 15)], ssem.at[S_C0])
    wait_all(y0.at[pl.ds(0, 15)], ssem.at[S_Y0])
    wait_all(vall.at[pl.ds(0, 15)], ssem.at[S_V])
    wait_all(rr.at[pl.ds(0, 15)], ssem.at[S_R])
    wait_all(r7.at[pl.ds(0, 15)], ssem.at[S_X0])
    for l in range(3):
        wait_all(s1.at[l, pl.ds(0, 15)], ssem.at[S_F1 + l])
        wait_all(s2.at[l, pl.ds(0, 15)], ssem.at[S_F2 + l])
        wait_all(r3.at[l, pl.ds(0, 15)], ssem.at[S_F3 + l])
        wait_all(rb1.at[l, pl.ds(0, 15)], ssem.at[S_B1 + l])
        wait_all(r4.at[l, pl.ds(0, 15)], ssem.at[S_B2 + l])
        if l > 0:
            wait_all(s5.at[l, pl.ds(0, 15)], ssem.at[S_B3 + l])
            wait_all(ro.at[l, pl.ds(0, 15)], ssem.at[S_OUT + l])
    for l in range(4):
        for m in range(4):
            @pl.when(c >= 4 * m)
            def _():
                wait_all(d_tile(l, m, pl.ds(0, 64 * 15)), dss.at[l, m])


def shards(rhs, diag_inv, panel, owner, target_block, row_map):
    code = (owner[:, 0, :, 0] * 8 + target_block[:, 0])[:, :, None] * 8 + jnp.arange(8, dtype=jnp.int32)
    code = jnp.pad(code.reshape(3, 112), ((0, 5), (0, 16)), constant_values=-1)
    vm = pl.BlockSpec(memory_space=pltpu.VMEM)
    b = lambda *s: pltpu.VMEM(s, BF16)
    f = lambda *s: pltpu.VMEM(s, F32)
    scratch = [
        b(3, 1792, 1024),
        b(4, 1024, 1024),
        b(1024, 2048),
        b(16, 64, 128), b(16, 64, 128),
        b(16, 32, 128), b(16, 32, 128), f(4, 64, 128),
        pltpu.VMEM((16, 8, 128), jnp.int32),
        b(4, 128, 1024), b(128, 1024),
        b(3, 16, 112, 128), b(3, 16, 128, 128),
        b(3, 16, 64, 128), b(3, 16, 64, 128),
        b(3, 64, 128), b(3, 16, 64, 128),
        b(3, 64, 128), b(3, 16, 64, 128),
        b(3, 16, 128, 128), b(3, 16, 112, 128),
        b(128, 1792), b(2048, 1024), b(128, 1024),
        b(3, 16, 64, 128), b(3, 16, 64, 128),
        f(3, 8, 8, 128), f(3, 16, 8, 128),
        b(16, 64, 128), b(16, 64, 128),
        f(128, 1024), f(128, 128),
        pltpu.SemaphoreType.DMA((3,)), pltpu.SemaphoreType.DMA((NSEM,)), pltpu.SemaphoreType.DMA((NSEM,)),
        pltpu.SemaphoreType.DMA((4, 4)), pltpu.SemaphoreType.DMA((4, 4)),
    ]
    got = pl.pallas_call(
        kernel,
        out_shape=jax.ShapeDtypeStruct((4, 64, 128), BF16),
        in_specs=[vm, vm, pl.BlockSpec(memory_space=pl.ANY), vm, vm],
        out_specs=vm,
        scratch_shapes=scratch,
        compiler_params=pltpu.CompilerParams(
            collective_id=0, has_side_effects=True, vmem_limit_bytes=58 << 20),
    )(rhs[:, 0], diag_inv[:, 0], panel[:, 0], code, row_map[:, 0])
    return got[:, None]


def solution(mesh):
    return jax.shard_map(
        shards,
        mesh=mesh,
        in_specs=(
            P(None, "prow", "pcol", None),
            P(None, "prow", "pcol", None),
            P(None, "prow", "pcol", None),
            P(None, "prow", "pcol", None),
            P(None, "prow", "pcol"),
            P(None, "prow", "pcol", None),
        ),
        out_specs=P(None, "prow", "pcol", None),
        check_vma=False,
    )
```

```python
import functools

import jax
import jax.numpy as jnp
from jax import lax
from jax.experimental import pallas as pl
from jax.experimental.pallas import tpu as pltpu
from jax.sharding import PartitionSpec as P

MESH = pl.DeviceIdType.MESH
N = 16
F32 = jnp.float32
BF16 = jnp.bfloat16


def nt(a, b):
    return lax.dot_general(a, b, (((1,), (1,)), ((), ())), preferred_element_type=F32)


def nn(a, b):
    return jnp.dot(a, b, preferred_element_type=F32)


S_C0, S_Y0, S_V, S_R, S_F1, S_F2, S_F3, S_B1, S_B2, S_B3, S_OUT, S_X0, S_G1, S_FS, S_BS = (
    0, 1, 2, 3, 4, 7, 10, 13, 16, 19, 22, 25, 26, 29, 32)
NSEM = 35


def kernel(rhs, dinv, panel_hbm, owner, tblock, rmap, out,
           panel, dfull, emat, c0, y0, sr, rr, rhsc, vall, yt, ct,
           s1, r1, s2, r2, s3, r3, sb1, rb1, s4, r4, gt, tt, wt, s5, r5, so, ro, s7, r7, xf, tile, wide, half, rsib, rbs, gacc,
           psem, ssem, rsem, dss, drs):
    p = lax.axis_index("prow")
    c = lax.axis_index("pcol")
    x, y = c // 4, c % 4

    def plane_dev(d):
        return (p, lax.rem(x + d // 4, 4) * 4 + lax.rem(y + d % 4, 4))

    z, k = p // 2, lax.rem(p, 2)
    sibling = (z * 2 + 1 - k, c)

    def z_dev(d):
        return (lax.rem(z + d, 8) * 2 + k, c)

    for l in range(3):
        pltpu.make_async_copy(panel_hbm.at[l], panel.at[l], psem.at[l]).start()

    bar = pltpu.get_barrier_semaphore()

    def greet(d, _):
        pl.semaphore_signal(bar, inc=1, device_id=plane_dev(d), device_id_type=MESH)
        return 0

    def greet_z(d, _):
        pl.semaphore_signal(bar, inc=1, device_id=z_dev(d), device_id_type=MESH)
        return 0

    c0[c] = rhs[0]
    r1[:, :, 112:128, :] = jnp.zeros((3, N, 16, 128), BF16)
    lax.fori_loop(1, N, greet, 0)
    lax.fori_loop(1, 8, greet_z, 0)
    pl.semaphore_signal(bar, inc=1, device_id=sibling, device_id_type=MESH)

    own = owner[:, 0, :]
    number = ((lax.rem(own, 2) * 8 + own // 2) * 8 + tblock[:, 0, :]).astype(F32)
    wide[...] = jnp.zeros((8, 128), F32)
    wide[0:3, 0:14] = number
    lane = lax.broadcasted_iota(jnp.int32, (8, 128), 1)
    repeat = (lax.broadcasted_iota(jnp.int32, (128, 128), 1) // 8 == lax.broadcasted_iota(jnp.int32, (128, 128), 0))
    repeated = nn(wide[...].astype(BF16), jnp.where(repeat, 1.0, 0.0).astype(BF16)).astype(jnp.int32)
    vall[c] = jnp.where(lane < 112, repeated * 8 + lax.rem(lane, 8), -1)
    for l in range(0, 4, 2):
        halves = []
        for q in (l, l + 1):
            r = rhs[q].astype(F32)
            halves.append(jnp.concatenate([r, r], axis=0).T.reshape(N, 8, 128))
        sr[:, l * 8:l * 8 + 16, :] = jnp.concatenate(halves, axis=1).astype(BF16)
    rr[c] = sr[c]
    pl.semaphore_wait(bar, 23)

    def spread(dev, src, dst, sem, count=N):
        def step(d, _):
            to = dev(d)
            pltpu.make_async_remote_copy(src(to), dst, ssem.at[sem], rsem.at[sem], device_id=to, device_id_type=MESH).start()
            return 0
        lax.fori_loop(1, count, step, 0)

    def remote(src, dst, to, sem):
        return pltpu.make_async_remote_copy(src, dst, ssem.at[sem], rsem.at[sem], device_id=to, device_id_type=MESH)

    def wait_all(ref, sem):
        pltpu.make_async_copy(ref, ref, sem).wait()

    spread(plane_dev, lambda to: c0.at[c], c0.at[c], S_C0)
    spread(plane_dev, lambda to: vall.at[c], vall.at[c], S_V)
    spread(plane_dev, lambda to: sr.at[to[1]], rr.at[c], S_R)
    wait_all(c0.at[pl.ds(0, 15)], rsem.at[S_C0])
    y0[c] = nn(dinv[0], c0[...].reshape(1024, 128)).astype(BF16)
    spread(plane_dev, lambda to: y0.at[c], y0.at[c], S_Y0)

    wait_all(rr.at[pl.ds(0, 15)], rsem.at[S_R])
    first = lax.broadcasted_iota(jnp.int32, (8, 128), 1) < 64
    for l in range(1, 4):
        for tb in range(8):
            a = rr[2 * tb, :, :].astype(F32)[8 * l:8 * l + 8]
            b = rr[2 * tb + 1, :, :].astype(F32)[8 * l:8 * l + 8]
            rhsc[l, tb * 8:tb * 8 + 8, :] = jnp.where(first, a, b)
    wait_all(vall.at[pl.ds(0, 15)], rsem.at[S_V])

    def build_e(l):
        rows = lax.broadcasted_iota(jnp.int32, (1024, 128), 0)

        def one(s, _):
            v = vall[s, pl.ds(l, 1), :]
            emat[:, pl.ds(pl.multiple_of(s * 128, 128), 128)] = jnp.where(rows == v, 1.0, 0.0).astype(BF16)
            return 0
        lax.fori_loop(0, N, one, 0)

    def build_et(l, ematt):
        lanes = lax.broadcasted_iota(jnp.int32, (128, 1024), 1).astype(F32)

        def one(s, _):
            v = jnp.broadcast_to(vall[s, pl.ds(l, 1), :].astype(F32), (128, 128)).T
            v = jnp.concatenate([v] * 8, axis=1)
            ematt[pl.ds(pl.multiple_of(s * 128, 128), 128), :] = jnp.where(lanes == v, 1.0, 0.0).astype(BF16)
            return 0
        lax.fori_loop(0, N, one, 0)

    def d_tile(l, m, rows):
        return dfull.at[l, m, rows, :]

    def x_dev(d):
        return (p, lax.rem(x + d, 4) * 4 + y)

    def y_dev(d):
        return (p, x * 4 + lax.rem(y + d, 4))

    def send_tile(l, leg, m, dev, rows):
        def step(d, _):
            pltpu.make_async_remote_copy(
                d_tile(l, m, rows), d_tile(l, m, rows), dss.at[l, leg * 4 + m], drs.at[l, leg * 4 + m],
                device_id=dev(d), device_id_type=MESH).start()
            return 0
        lax.fori_loop(1, 4, step, 0)

    def wait_tiles(sems, l, leg, m, tiles):
        wait_all(d_tile(l, m, pl.ds(0, 64 * tiles)), sems.at[l, leg * 4 + m])

    def start_d(l):
        mine = pl.ds(pl.multiple_of(c * 64, 64), 64)
        for m in range(4):
            dfull[l, m, mine, :] = dinv[l, :, m * 256:m * 256 + 256]
        for m, dev in ((0, x_dev), (1, y_dev), (2, y_dev), (3, x_dev)):
            @pl.when(x >= m)
            def _():
                send_tile(l, 0, m, dev, mine)

    def forward_d(l):
        wait_tiles(drs, l, 0, 0, 3)

        @pl.when(x < 3)
        def _():
            wait_tiles(drs, l, 0, 3, 1)

        def chunk(g, _):
            send_tile(l, 1, 0, y_dev, pl.ds(pl.multiple_of((g * 4 + y) * 64, 64), 64))
            return 0
        lax.fori_loop(0, 4, chunk, 0)
        send_tile(l, 1, 3, y_dev, pl.ds(pl.multiple_of((12 + y) * 64, 64), 64))
        for m in (1, 2):
            @pl.when(x >= m)
            def _():
                wait_tiles(drs, l, 0, m, 3)
                send_tile(l, 1, m, x_dev, pl.ds(pl.multiple_of(x * 256, 256), 256))

    def wait_d(l):
        wait_tiles(drs, l, 1, 0, 12)
        wait_tiles(drs, l, 1, 3, 3)
        for m in (1, 2):
            @pl.when(x >= m)
            def _():
                wait_tiles(drs, l, 1, m, 4 * (3 - m))

            @pl.when(x < m)
            def _():
                wait_tiles(drs, l, 1, m, 4 * (4 - m))

    def place(l, b):
        rows = lax.broadcasted_iota(jnp.int32, (128, 128), 0)
        return jnp.where(rows == rmap[l, b], 1.0, 0.0).astype(BF16)

    wait_all(y0.at[pl.ds(0, 15)], rsem.at[S_Y0])
    for i in range(8):
        yt[0, :, i * 128:i * 128 + 128] = y0[2 * i:2 * i + 2].reshape(128, 128).astype(F32).T.astype(BF16)

    def forward(l, _):
        pltpu.make_async_copy(panel_hbm.at[l], panel.at[l], psem.at[l]).wait()

        def pair(n, _):
            u = nt(yt[l], panel[l, n * 256:n * 256 + 256, :]).astype(BF16)
            a = nt(u[:, :128], place(l, 2 * n)).reshape(N, 8, 128)
            b = nt(u[:, 128:], place(l, 2 * n + 1)).reshape(N, 8, 128)
            s1[l, :, n * 16:n * 16 + 16, :] = jnp.concatenate([a, b], axis=1).astype(BF16)
            return 0
        for n in range(4):
            pair(n, 0)
        early, late = pl.ds(0, 64), pl.ds(64, 48)
        spread(plane_dev, lambda to: s1.at[l, to[1], early, :], r1.at[l, c, early, :], S_F1 + l)
        for n in range(4, 7):
            pair(n, 0)
        spread(plane_dev, lambda to: s1.at[l, to[1], late, :], r1.at[l, c, late, :], S_G1 + l)
        r1[l, c, 0:112, :] = s1[l, c]
        build_e(l)
        start_d(l + 1)
        wait_all(r1.at[l, pl.ds(0, 15), early, :], rsem.at[S_F1 + l])
        wait_all(r1.at[l, pl.ds(0, 15), late, :], rsem.at[S_G1 + l])

        forward_d(l + 1)

        def owners(parity, q):
            rows = pl.ds(pl.multiple_of(parity * 512 + q * 256, 256), 256)
            return nn(emat[rows, :], r1[l].reshape(2048, 128)).reshape(4, 64, 128)
        for q in range(2):
            s2[l, 8 + q * 4:12 + q * 4] = owners(1 - k, q).astype(BF16)
        to_sibling = remote(s2.at[l, pl.ds(8, 8)], rsib.at[l], sibling, S_FS + l)
        to_sibling.start()
        for q in range(2):
            half[q * 4:q * 4 + 4] = owners(k, q)
        to_sibling.wait_recv()
        s2[l, 0:8] = (half[...] + rsib[l].astype(F32)).astype(BF16)
        r2[l, z] = s2[l, z]
        spread(z_dev, lambda to: s2.at[l, to[0] // 2], r2.at[l, z], S_F2 + l, 8)
        wait_all(r2.at[l, pl.ds(0, 7)], rsem.at[S_F2 + l])
        carried = jnp.sum(r2[l].astype(F32), axis=0)
        s3[l] = (rhsc[l + 1] - carried).astype(BF16)
        r3[l, c] = s3[l]
        spread(plane_dev, lambda to: s3.at[l], r3.at[l, c], S_F3 + l)
        wait_all(r3.at[l, pl.ds(0, 15)], rsem.at[S_F3 + l])
        got = r3[l].astype(F32).reshape(N, 8, 8, 128)
        for tb in range(8):
            ct[:, tb * 128:tb * 128 + 128] = got[:, tb].reshape(128, 128).astype(BF16)
        wait_d(l + 1)
        for i in range(4):
            e = 256 * (i + 1)
            yt[l + 1, :, i * 256:e] = sum(
                nt(ct[:, m * 256:m * 256 + 256], dfull[l + 1, m, i * 256:e, :]) for m in range(i + 1)).astype(BF16)
        return 0

    lax.fori_loop(0, 3, forward, 0)

    def back_solve(l):
        for m in range(4):
            xf[:, m * 256:m * 256 + 256] = nn(wt[:, m * 256:], dfull[l, m, m * 256:, :])

    def my_rows(tile_value):
        tile[...] = tile_value.T
        return tile[pl.ds(pl.multiple_of(lax.rem(c, 2) * 64, 64), 64), :].astype(BF16)

    wt[...] = yt[3]
    back_solve(3)
    mine8 = pl.ds(pl.multiple_of(c * 8, 8), 8)
    for tb in range(0, 8, 2):
        sb1[2, tb * 8:tb * 8 + 16, :] = jnp.concatenate(
            [xf[mine8, tb * 128:tb * 128 + 128], xf[mine8, tb * 128 + 128:tb * 128 + 256]], axis=0).astype(BF16)
    my_tile = c // 2

    def backward_to_partials(l):
        rb1[l, z] = sb1[l]
        spread(z_dev, lambda to: sb1.at[l], rb1.at[l, z], S_B1 + l, 8)
        build_et(l, ematt=emat_t)
        if not isinstance(l, int):
            @pl.when(l == 2)
            def _():
                start_d(0)

            @pl.when(l == 1)
            def _():
                forward_d(0)
        wait_all(rb1.at[l, pl.ds(0, 7)], rsem.at[S_B1 + l])
        to_sibling = remote(rb1.at[l], rbs.at[l], sibling, S_BS + l)
        to_sibling.start()
        mine = pl.ds(pl.multiple_of(k * 512, 512), 512)
        others = pl.ds(pl.multiple_of((1 - k) * 512, 512), 512)
        for n in range(4):
            gacc[n * 512:n * 512 + 512, :] = nn(emat_t[n * 512:n * 512 + 512, mine], rb1[l].reshape(512, 128))
        to_sibling.wait_recv()

        def holders(n, _):
            pair = lax.rem(c // 2 + n, 8)
            rows = pl.ds(pl.multiple_of(pair * 256, 256), 256)
            value = gacc[rows, :] + nn(emat_t[rows, others], rbs[l].reshape(512, 128))
            s4[l, pl.ds(pair * 2, 2)] = value.astype(BF16).reshape(2, 128, 128)
            for q in range(2):
                to = pair * 2 + q

                @pl.when(to != c)
                def _():
                    remote(s4.at[l, to, pl.ds(0, 112), :], r4.at[l, c], (p, to), S_B2 + l).start()
            return 0
        lax.fori_loop(0, 8, holders, 0)
        r4[l, c] = s4[l, c, 0:112, :]

    def backward_rest(l):
        wait_all(r4.at[l, pl.ds(0, 15)], rsem.at[S_B2 + l])

        def pair(n, _):
            got = r4[l, :, n * 16:n * 16 + 16, :].astype(F32)
            a = nn(got[:, :8].reshape(128, 128).astype(BF16), place(l, 2 * n))
            b = nn(got[:, 8:].reshape(128, 128).astype(BF16), place(l, 2 * n + 1))
            gt[:, n * 256:n * 256 + 256] = jnp.concatenate([a, b], axis=1).astype(BF16)
            return 0
        for n in range(7):
            pair(n, 0)

        def columns(n, _):
            cols = slice(n * 256, n * 256 + 256)
            t = nn(gt[...], panel[l, :, cols])
            wt[:, cols] = (yt[l, :, cols].astype(F32) * (1.0 / 16) - t).astype(BF16)
            return 0
        for n in range(4):
            columns(n, 0)
        back_solve(l)

    emat_t = tt

    def backward(m, _):
        l = 2 - m
        backward_to_partials(l)

        backward_rest(l)
        for tb in range(0, 8, 2):
            a = xf[:, tb * 128:tb * 128 + 128].reshape(N, 8, 128)
            b = xf[:, tb * 128 + 128:tb * 128 + 256].reshape(N, 8, 128)
            s5[l, :, tb * 8:tb * 8 + 16, :] = jnp.concatenate([a, b], axis=1).astype(BF16)
        r5[l, c] = s5[l, c]
        spread(plane_dev, lambda to: s5.at[l, to[1]], r5.at[l, c], S_B3 + l)
        wait_all(r5.at[l, pl.ds(0, 15)], rsem.at[S_B3 + l])
        total = jnp.sum(r5[l].astype(F32), axis=0).astype(BF16)
        sb1[l - 1] = total
        so[l] = total.astype(F32).reshape(8, 8, 128)
        ro[l, c] = so[l, my_tile]
        spread(plane_dev, lambda to: so.at[l, to[1] // 2], ro.at[l, c], S_OUT + l)
        return 0

    out[3] = my_rows(xf[:, pl.ds(pl.multiple_of(my_tile * 128, 128), 128)])
    lax.fori_loop(0, 2, backward, 0)
    backward_to_partials(0)
    for l in (2, 1):
        wait_all(ro.at[l, pl.ds(0, 15)], rsem.at[S_OUT + l])
        out[l] = my_rows(ro[l].reshape(128, 128))
    wait_d(0)
    backward_rest(0)
    for i in range(8):
        s7[2 * i:2 * i + 2] = xf[:, i * 128:i * 128 + 128].T.astype(BF16).reshape(2, 64, 128)
    r7[c] = s7[c]
    spread(plane_dev, lambda to: s7.at[to[1]], r7.at[c], S_X0)
    wait_all(r7.at[pl.ds(0, 15)], rsem.at[S_X0])
    out[0] = jnp.sum(r7[...].astype(F32), axis=0).astype(BF16)

    wait_all(c0.at[pl.ds(0, 15)], ssem.at[S_C0])
    wait_all(y0.at[pl.ds(0, 15)], ssem.at[S_Y0])
    wait_all(vall.at[pl.ds(0, 15)], ssem.at[S_V])
    wait_all(rr.at[pl.ds(0, 15)], ssem.at[S_R])
    wait_all(r7.at[pl.ds(0, 15)], ssem.at[S_X0])
    for l in range(3):
        wait_all(s1.at[l, pl.ds(0, 15), pl.ds(0, 64), :], ssem.at[S_F1 + l])
        wait_all(s1.at[l, pl.ds(0, 15), pl.ds(64, 48), :], ssem.at[S_G1 + l])
        wait_all(rsib.at[l], ssem.at[S_FS + l])
        wait_all(rbs.at[l], ssem.at[S_BS + l])
        wait_all(r2.at[l, pl.ds(0, 7)], ssem.at[S_F2 + l])
        wait_all(r3.at[l, pl.ds(0, 15)], ssem.at[S_F3 + l])
        wait_all(rb1.at[l, pl.ds(0, 7)], ssem.at[S_B1 + l])
        wait_all(r4.at[l, pl.ds(0, 15)], ssem.at[S_B2 + l])
        if l > 0:
            wait_all(s5.at[l, pl.ds(0, 15)], ssem.at[S_B3 + l])
            wait_all(ro.at[l, pl.ds(0, 15)], ssem.at[S_OUT + l])
    for l in range(4):
        wait_tiles(dss, l, 1, 0, 12)
        wait_tiles(dss, l, 1, 3, 3)
        for m in range(4):
            @pl.when(x >= m)
            def _():
                wait_tiles(dss, l, 0, m, 3)
                if m in (1, 2):
                    wait_tiles(dss, l, 1, m, 12)


def shards(rhs, diag_inv, panel, owner, target_block, row_map):
    vm = pl.BlockSpec(memory_space=pltpu.VMEM)
    b = lambda *s: pltpu.VMEM(s, BF16)
    f = lambda *s: pltpu.VMEM(s, F32)
    scratch = [
        b(3, 1792, 1024),
        b(4, 4, 1024, 256),
        b(1024, 2048),
        b(16, 64, 128), b(16, 64, 128),
        b(16, 32, 128), b(16, 32, 128), f(4, 64, 128),
        pltpu.VMEM((16, 8, 128), jnp.int32),
        b(4, 128, 1024), b(128, 1024),
        b(3, 16, 112, 128), b(3, 16, 128, 128),
        b(3, 16, 64, 128), b(3, 8, 64, 128),
        b(3, 64, 128), b(3, 16, 64, 128),
        b(3, 64, 128), b(3, 8, 64, 128),
        b(3, 16, 128, 128), b(3, 16, 112, 128),
        b(128, 1792), b(2048, 1024), b(128, 1024),
        b(3, 16, 64, 128), b(3, 16, 64, 128),
        f(3, 8, 8, 128), f(3, 16, 8, 128),
        b(16, 64, 128), b(16, 64, 128),
        f(128, 1024), f(128, 128), f(8, 128), f(8, 64, 128),
        b(3, 8, 64, 128), b(3, 8, 64, 128), f(2048, 128),
        pltpu.SemaphoreType.DMA((3,)), pltpu.SemaphoreType.DMA((NSEM,)), pltpu.SemaphoreType.DMA((NSEM,)),
        pltpu.SemaphoreType.DMA((4, 8)), pltpu.SemaphoreType.DMA((4, 8)),
    ]
    got = pl.pallas_call(
        kernel,
        out_shape=jax.ShapeDtypeStruct((4, 64, 128), BF16),
        in_specs=[vm, vm, pl.BlockSpec(memory_space=pl.ANY), vm, vm, vm],
        out_specs=vm,
        scratch_shapes=scratch,
        compiler_params=pltpu.CompilerParams(
            collective_id=0, has_side_effects=True, vmem_limit_bytes=58 << 20),
    )(rhs[:, 0], diag_inv[:, 0], panel[:, 0], owner.reshape(3, 1, 14), target_block, jnp.transpose(row_map, (0, 2, 1, 3)))
    return got[:, None]


def solution(mesh):
    return jax.shard_map(
        shards,
        mesh=mesh,
        in_specs=(
            P(None, "prow", "pcol", None),
            P(None, "prow", "pcol", None),
            P(None, "prow", "pcol", None),
            P(None, "prow", "pcol", None),
            P(None, "prow", "pcol"),
            P(None, "prow", "pcol", None),
        ),
        out_specs=P(None, "prow", "pcol", None),
        check_vma=False,
    )
```

```python
import functools

import jax
import jax.numpy as jnp
from jax import lax
from jax.experimental import pallas as pl
from jax.experimental.pallas import tpu as pltpu
from jax.sharding import PartitionSpec as P

MESH = pl.DeviceIdType.MESH
N = 16
F32 = jnp.float32
BF16 = jnp.bfloat16


def nt(a, b):
    return lax.dot_general(a, b, (((1,), (1,)), ((), ())), preferred_element_type=F32)


def nn(a, b):
    return jnp.dot(a, b, preferred_element_type=F32)


S_C0, S_Y0, S_V, S_R, S_F1, S_F2, S_F3, S_B1, S_B2, S_B3, S_OUT, S_X0, S_G1, S_FS, S_BS = (
    0, 1, 2, 3, 4, 7, 10, 13, 16, 19, 22, 25, 26, 29, 32)
NSEM = 35


def kernel(rhs, dinv, panel_hbm, owner, tblock, rmap, out,
           panel, dfull, emat, c0, y0, sr, rr, rhsc, vall, yt, ct,
           s1, r1, s2, r2, s3, r3, sb1, rb1, s4, r4, gt, tt, wt, s5, r5, so, ro, s7, r7, xf, tile, wide, half, rsib, rbs, gacc,
           psem, ssem, rsem, dss, drs):
    p = lax.axis_index("prow")
    c = lax.axis_index("pcol")
    x, y = c // 4, c % 4

    def plane_dev(d):
        return (p, lax.rem(x + d // 4, 4) * 4 + lax.rem(y + d % 4, 4))

    z, k = p // 2, lax.rem(p, 2)
    sibling = (z * 2 + 1 - k, c)

    def z_dev(d):
        return (lax.rem(z + d, 8) * 2 + k, c)

    for l in range(3):
        pltpu.make_async_copy(panel_hbm.at[l], panel.at[l], psem.at[l]).start()

    bar = pltpu.get_barrier_semaphore()

    def greet(d, _):
        pl.semaphore_signal(bar, inc=1, device_id=plane_dev(d), device_id_type=MESH)
        return 0

    def greet_z(d, _):
        pl.semaphore_signal(bar, inc=1, device_id=z_dev(d), device_id_type=MESH)
        return 0

    c0[c] = rhs[0]
    r1[:, :, 112:128, :] = jnp.zeros((3, N, 16, 128), BF16)
    lax.fori_loop(1, N, greet, 0)
    lax.fori_loop(1, 8, greet_z, 0)
    pl.semaphore_signal(bar, inc=1, device_id=sibling, device_id_type=MESH)

    own = owner[:, 0, :]
    number = ((lax.rem(own, 2) * 8 + own // 2) * 8 + tblock[:, 0, :]).astype(F32)
    wide[...] = jnp.zeros((8, 128), F32)
    wide[0:3, 0:14] = number
    lane = lax.broadcasted_iota(jnp.int32, (8, 128), 1)
    repeat = (lax.broadcasted_iota(jnp.int32, (128, 128), 1) // 8 == lax.broadcasted_iota(jnp.int32, (128, 128), 0))
    repeated = nn(wide[...].astype(BF16), jnp.where(repeat, 1.0, 0.0).astype(BF16)).astype(jnp.int32)
    vall[c] = jnp.where(lane < 112, repeated * 8 + lax.rem(lane, 8), -1)
    for l in range(0, 4, 2):
        halves = []
        for q in (l, l + 1):
            r = rhs[q].astype(F32)
            halves.append(jnp.concatenate([r, r], axis=0).T.reshape(N, 8, 128))
        sr[:, l * 8:l * 8 + 16, :] = jnp.concatenate(halves, axis=1).astype(BF16)
    rr[c] = sr[c]
    pl.semaphore_wait(bar, 23)

    def spread(dev, src, dst, sem, count=N):
        def step(d, _):
            to = dev(d)
            pltpu.make_async_remote_copy(src(to), dst, ssem.at[sem], rsem.at[sem], device_id=to, device_id_type=MESH).start()
            return 0
        lax.fori_loop(1, count, step, 0)

    def remote(src, dst, to, sem):
        return pltpu.make_async_remote_copy(src, dst, ssem.at[sem], rsem.at[sem], device_id=to, device_id_type=MESH)

    def wait_all(ref, sem):
        pltpu.make_async_copy(ref, ref, sem).wait()

    spread(plane_dev, lambda to: c0.at[c], c0.at[c], S_C0)
    spread(plane_dev, lambda to: vall.at[c], vall.at[c], S_V)
    spread(plane_dev, lambda to: sr.at[to[1]], rr.at[c], S_R)

    def place_rows(l):
        pltpu.make_async_copy(panel_hbm.at[l], panel.at[l], psem.at[l]).wait()
        rows = lax.broadcasted_iota(jnp.int32, (128, 128), 0)

        def one(b, _):
            block = pl.ds(pl.multiple_of(b * 128, 128), 128)
            placed = jnp.where(rows == rmap[l, b], 1.0, 0.0).astype(BF16)
            panel[l, block, :] = nn(placed, panel[l, block, :]).astype(BF16)
            return 0
        lax.fori_loop(0, 14, one, 0)

    place_rows(0)
    wait_all(c0.at[pl.ds(0, 15)], rsem.at[S_C0])
    y0[c] = nn(dinv[0], c0[...].reshape(1024, 128)).astype(BF16)
    spread(plane_dev, lambda to: y0.at[c], y0.at[c], S_Y0)

    wait_all(rr.at[pl.ds(0, 15)], rsem.at[S_R])
    first = lax.broadcasted_iota(jnp.int32, (8, 128), 1) < 64
    for l in range(1, 4):
        for tb in range(8):
            a = rr[2 * tb, :, :].astype(F32)[8 * l:8 * l + 8]
            b = rr[2 * tb + 1, :, :].astype(F32)[8 * l:8 * l + 8]
            rhsc[l, tb * 8:tb * 8 + 8, :] = jnp.where(first, a, b)
    wait_all(vall.at[pl.ds(0, 15)], rsem.at[S_V])

    def build_e(l):
        rows = lax.broadcasted_iota(jnp.int32, (1024, 128), 0)

        def one(s, _):
            v = vall[s, pl.ds(l, 1), :]
            emat[:, pl.ds(pl.multiple_of(s * 128, 128), 128)] = jnp.where(rows == v, 1.0, 0.0).astype(BF16)
            return 0
        lax.fori_loop(0, N, one, 0)

    def build_et(l, ematt):
        lanes = lax.broadcasted_iota(jnp.int32, (128, 1024), 1).astype(F32)

        def one(s, _):
            v = jnp.broadcast_to(vall[s, pl.ds(l, 1), :].astype(F32), (128, 128)).T
            v = jnp.concatenate([v] * 8, axis=1)
            ematt[pl.ds(pl.multiple_of(s * 128, 128), 128), :] = jnp.where(lanes == v, 1.0, 0.0).astype(BF16)
            return 0
        lax.fori_loop(0, N, one, 0)

    def d_tile(l, m, rows):
        return dfull.at[l, m, rows, :]

    def x_dev(d):
        return (p, lax.rem(x + d, 4) * 4 + y)

    def y_dev(d):
        return (p, x * 4 + lax.rem(y + d, 4))

    def send_tile(l, leg, m, dev, rows):
        def step(d, _):
            pltpu.make_async_remote_copy(
                d_tile(l, m, rows), d_tile(l, m, rows), dss.at[l, leg * 4 + m], drs.at[l, leg * 4 + m],
                device_id=dev(d), device_id_type=MESH).start()
            return 0
        lax.fori_loop(1, 4, step, 0)

    def wait_tiles(sems, l, leg, m, tiles):
        wait_all(d_tile(l, m, pl.ds(0, 64 * tiles)), sems.at[l, leg * 4 + m])

    def start_d(l):
        mine = pl.ds(pl.multiple_of(c * 64, 64), 64)
        for m in range(4):
            dfull[l, m, mine, :] = dinv[l, :, m * 256:m * 256 + 256]
        for m, dev in ((0, x_dev), (1, y_dev), (2, y_dev), (3, x_dev)):
            @pl.when(x >= m)
            def _():
                send_tile(l, 0, m, dev, mine)

    def forward_d(l):
        wait_tiles(drs, l, 0, 0, 3)

        @pl.when(x < 3)
        def _():
            wait_tiles(drs, l, 0, 3, 1)

        def chunk(g, _):
            send_tile(l, 1, 0, y_dev, pl.ds(pl.multiple_of((g * 4 + y) * 64, 64), 64))
            return 0
        lax.fori_loop(0, 4, chunk, 0)
        send_tile(l, 1, 3, y_dev, pl.ds(pl.multiple_of((12 + y) * 64, 64), 64))
        for m in (1, 2):
            @pl.when(x >= m)
            def _():
                wait_tiles(drs, l, 0, m, 3)
                send_tile(l, 1, m, x_dev, pl.ds(pl.multiple_of(x * 256, 256), 256))

    def wait_d(l):
        wait_tiles(drs, l, 1, 0, 12)
        wait_tiles(drs, l, 1, 3, 3)
        for m in (1, 2):
            @pl.when(x >= m)
            def _():
                wait_tiles(drs, l, 1, m, 4 * (3 - m))

            @pl.when(x < m)
            def _():
                wait_tiles(drs, l, 1, m, 4 * (4 - m))

    wait_all(y0.at[pl.ds(0, 15)], rsem.at[S_Y0])
    start_d(1)
    for i in range(8):
        yt[0, :, i * 128:i * 128 + 128] = y0[2 * i:2 * i + 2].reshape(128, 128).astype(F32).T.astype(BF16)

    def forward(l, _):
        def pair(n, _):
            u = nt(yt[l], panel[l, n * 256:n * 256 + 256, :])
            a = u[:, :128].reshape(N, 8, 128)
            b = u[:, 128:].reshape(N, 8, 128)
            s1[l, :, n * 16:n * 16 + 16, :] = jnp.concatenate([a, b], axis=1).astype(BF16)
            return 0
        for n in range(4):
            pair(n, 0)
        early, late = pl.ds(0, 64), pl.ds(64, 48)
        spread(plane_dev, lambda to: s1.at[l, to[1], early, :], r1.at[l, c, early, :], S_F1 + l)
        for n in range(4, 7):
            pair(n, 0)
        spread(plane_dev, lambda to: s1.at[l, to[1], late, :], r1.at[l, c, late, :], S_G1 + l)
        r1[l, c, 0:112, :] = s1[l, c]
        build_e(l)
        wait_all(r1.at[l, pl.ds(0, 15), early, :], rsem.at[S_F1 + l])
        wait_all(r1.at[l, pl.ds(0, 15), late, :], rsem.at[S_G1 + l])


        def owners(parity, q):
            rows = pl.ds(pl.multiple_of(parity * 512 + q * 256, 256), 256)
            return nn(emat[rows, :], r1[l].reshape(2048, 128)).reshape(4, 64, 128)
        for q in range(2):
            s2[l, 8 + q * 4:12 + q * 4] = owners(1 - k, q).astype(BF16)
        to_sibling = remote(s2.at[l, pl.ds(8, 8)], rsib.at[l], sibling, S_FS + l)
        to_sibling.start()
        forward_d(l + 1)
        for q in range(2):
            half[q * 4:q * 4 + 4] = owners(k, q)
        to_sibling.wait_recv()
        s2[l, 0:8] = (half[...] + rsib[l].astype(F32)).astype(BF16)
        r2[l, z] = s2[l, z]
        spread(z_dev, lambda to: s2.at[l, to[0] // 2], r2.at[l, z], S_F2 + l, 8)

        @pl.when(l < 2)
        def _():
            place_rows(l + 1)
        wait_all(r2.at[l, pl.ds(0, 7)], rsem.at[S_F2 + l])
        carried = jnp.sum(r2[l].astype(F32), axis=0)
        s3[l] = (rhsc[l + 1] - carried).astype(BF16)
        r3[l, c] = s3[l]
        spread(plane_dev, lambda to: s3.at[l], r3.at[l, c], S_F3 + l)
        wait_all(r3.at[l, pl.ds(0, 15)], rsem.at[S_F3 + l])
        start_d(lax.rem(l + 2, 4))
        got = r3[l].astype(F32).reshape(N, 8, 8, 128)
        for tb in range(8):
            ct[:, tb * 128:tb * 128 + 128] = got[:, tb].reshape(128, 128).astype(BF16)
        wait_d(l + 1)
        for i in range(4):
            e = 256 * (i + 1)
            yt[l + 1, :, i * 256:e] = sum(
                nt(ct[:, m * 256:m * 256 + 256], dfull[l + 1, m, i * 256:e, :]) for m in range(i + 1)).astype(BF16)
        return 0

    lax.fori_loop(0, 3, forward, 0)

    def back_solve(l):
        for m in range(4):
            xf[:, m * 256:m * 256 + 256] = nn(wt[:, m * 256:], dfull[l, m, m * 256:, :])

    def my_rows(tile_value):
        tile[...] = tile_value.T
        return tile[pl.ds(pl.multiple_of(lax.rem(c, 2) * 64, 64), 64), :].astype(BF16)

    wt[...] = yt[3]
    back_solve(3)
    mine8 = pl.ds(pl.multiple_of(c * 8, 8), 8)
    for tb in range(0, 8, 2):
        sb1[2, tb * 8:tb * 8 + 16, :] = jnp.concatenate(
            [xf[mine8, tb * 128:tb * 128 + 128], xf[mine8, tb * 128 + 128:tb * 128 + 256]], axis=0).astype(BF16)
    my_tile = c // 2

    def backward_to_partials(l):
        rb1[l, z] = sb1[l]
        spread(z_dev, lambda to: sb1.at[l], rb1.at[l, z], S_B1 + l, 8)
        build_et(l, ematt=emat_t)
        if not isinstance(l, int):
            @pl.when(l == 1)
            def _():
                forward_d(0)
        wait_all(rb1.at[l, pl.ds(0, 7)], rsem.at[S_B1 + l])
        to_sibling = remote(rb1.at[l], rbs.at[l], sibling, S_BS + l)
        to_sibling.start()
        mine = pl.ds(pl.multiple_of(k * 512, 512), 512)
        others = pl.ds(pl.multiple_of((1 - k) * 512, 512), 512)
        for n in range(4):
            gacc[n * 512:n * 512 + 512, :] = nn(emat_t[n * 512:n * 512 + 512, mine], rb1[l].reshape(512, 128))
        to_sibling.wait_recv()

        def holders(n, _):
            pair = lax.rem(c // 2 + n, 8)
            rows = pl.ds(pl.multiple_of(pair * 256, 256), 256)
            value = gacc[rows, :] + nn(emat_t[rows, others], rbs[l].reshape(512, 128))
            s4[l, pl.ds(pair * 2, 2)] = value.astype(BF16).reshape(2, 128, 128)
            for q in range(2):
                to = pair * 2 + q

                @pl.when(to != c)
                def _():
                    remote(s4.at[l, to, pl.ds(0, 112), :], r4.at[l, c], (p, to), S_B2 + l).start()
            return 0
        lax.fori_loop(0, 8, holders, 0)
        r4[l, c] = s4[l, c, 0:112, :]

    def backward_rest(l):
        wait_all(r4.at[l, pl.ds(0, 15)], rsem.at[S_B2 + l])

        def pair(n, _):
            got = r4[l, :, n * 16:n * 16 + 16, :].astype(F32)
            a = got[:, :8].reshape(128, 128)
            b = got[:, 8:].reshape(128, 128)
            gt[:, n * 256:n * 256 + 256] = jnp.concatenate([a, b], axis=1).astype(BF16)
            return 0
        for n in range(7):
            pair(n, 0)

        def columns(n, _):
            cols = slice(n * 256, n * 256 + 256)
            t = nn(gt[...], panel[l, :, cols])
            wt[:, cols] = (yt[l, :, cols].astype(F32) * (1.0 / 16) - t).astype(BF16)
            return 0
        for n in range(4):
            columns(n, 0)
        back_solve(l)

    emat_t = tt

    def backward(m, _):
        l = 2 - m
        backward_to_partials(l)

        backward_rest(l)
        for tb in range(0, 8, 2):
            a = xf[:, tb * 128:tb * 128 + 128].reshape(N, 8, 128)
            b = xf[:, tb * 128 + 128:tb * 128 + 256].reshape(N, 8, 128)
            s5[l, :, tb * 8:tb * 8 + 16, :] = jnp.concatenate([a, b], axis=1).astype(BF16)
        r5[l, c] = s5[l, c]
        spread(plane_dev, lambda to: s5.at[l, to[1]], r5.at[l, c], S_B3 + l)
        wait_all(r5.at[l, pl.ds(0, 15)], rsem.at[S_B3 + l])
        total = jnp.sum(r5[l].astype(F32), axis=0).astype(BF16)
        sb1[l - 1] = total
        so[l] = total.astype(F32).reshape(8, 8, 128)
        ro[l, c] = so[l, my_tile]
        spread(plane_dev, lambda to: so.at[l, to[1] // 2], ro.at[l, c], S_OUT + l)
        return 0

    out[3] = my_rows(xf[:, pl.ds(pl.multiple_of(my_tile * 128, 128), 128)])
    lax.fori_loop(0, 2, backward, 0)
    backward_to_partials(0)
    for l in (2, 1):
        wait_all(ro.at[l, pl.ds(0, 15)], rsem.at[S_OUT + l])
        out[l] = my_rows(ro[l].reshape(128, 128))
    wait_d(0)
    backward_rest(0)
    for i in range(8):
        s7[2 * i:2 * i + 2] = xf[:, i * 128:i * 128 + 128].T.astype(BF16).reshape(2, 64, 128)
    r7[c] = s7[c]
    spread(plane_dev, lambda to: s7.at[to[1]], r7.at[c], S_X0)
    wait_all(r7.at[pl.ds(0, 15)], rsem.at[S_X0])
    out[0] = jnp.sum(r7[...].astype(F32), axis=0).astype(BF16)

    wait_all(c0.at[pl.ds(0, 15)], ssem.at[S_C0])
    wait_all(y0.at[pl.ds(0, 15)], ssem.at[S_Y0])
    wait_all(vall.at[pl.ds(0, 15)], ssem.at[S_V])
    wait_all(rr.at[pl.ds(0, 15)], ssem.at[S_R])
    wait_all(r7.at[pl.ds(0, 15)], ssem.at[S_X0])
    for l in range(3):
        wait_all(s1.at[l, pl.ds(0, 15), pl.ds(0, 64), :], ssem.at[S_F1 + l])
        wait_all(s1.at[l, pl.ds(0, 15), pl.ds(64, 48), :], ssem.at[S_G1 + l])
        wait_all(rsib.at[l], ssem.at[S_FS + l])
        wait_all(rbs.at[l], ssem.at[S_BS + l])
        wait_all(r2.at[l, pl.ds(0, 7)], ssem.at[S_F2 + l])
        wait_all(r3.at[l, pl.ds(0, 15)], ssem.at[S_F3 + l])
        wait_all(rb1.at[l, pl.ds(0, 7)], ssem.at[S_B1 + l])
        wait_all(r4.at[l, pl.ds(0, 15)], ssem.at[S_B2 + l])
        if l > 0:
            wait_all(s5.at[l, pl.ds(0, 15)], ssem.at[S_B3 + l])
            wait_all(ro.at[l, pl.ds(0, 15)], ssem.at[S_OUT + l])
    for l in range(4):
        wait_tiles(dss, l, 1, 0, 12)
        wait_tiles(dss, l, 1, 3, 3)
        for m in range(4):
            @pl.when(x >= m)
            def _():
                wait_tiles(dss, l, 0, m, 3)
                if m in (1, 2):
                    wait_tiles(dss, l, 1, m, 12)


def shards(rhs, diag_inv, panel, owner, target_block, row_map):
    vm = pl.BlockSpec(memory_space=pltpu.VMEM)
    b = lambda *s: pltpu.VMEM(s, BF16)
    f = lambda *s: pltpu.VMEM(s, F32)
    scratch = [
        b(3, 1792, 1024),
        b(4, 4, 1024, 256),
        b(1024, 2048),
        b(16, 64, 128), b(16, 64, 128),
        b(16, 32, 128), b(16, 32, 128), f(4, 64, 128),
        pltpu.VMEM((16, 8, 128), jnp.int32),
        b(4, 128, 1024), b(128, 1024),
        b(3, 16, 112, 128), b(3, 16, 128, 128),
        b(3, 16, 64, 128), b(3, 8, 64, 128),
        b(3, 64, 128), b(3, 16, 64, 128),
        b(3, 64, 128), b(3, 8, 64, 128),
        b(3, 16, 128, 128), b(3, 16, 112, 128),
        b(128, 1792), b(2048, 1024), b(128, 1024),
        b(3, 16, 64, 128), b(3, 16, 64, 128),
        f(3, 8, 8, 128), f(3, 16, 8, 128),
        b(16, 64, 128), b(16, 64, 128),
        f(128, 1024), f(128, 128), f(8, 128), f(8, 64, 128),
        b(3, 8, 64, 128), b(3, 8, 64, 128), f(2048, 128),
        pltpu.SemaphoreType.DMA((3,)), pltpu.SemaphoreType.DMA((NSEM,)), pltpu.SemaphoreType.DMA((NSEM,)),
        pltpu.SemaphoreType.DMA((4, 8)), pltpu.SemaphoreType.DMA((4, 8)),
    ]
    got = pl.pallas_call(
        kernel,
        out_shape=jax.ShapeDtypeStruct((4, 64, 128), BF16),
        in_specs=[vm, vm, pl.BlockSpec(memory_space=pl.ANY), vm, vm, vm],
        out_specs=vm,
        scratch_shapes=scratch,
        compiler_params=pltpu.CompilerParams(
            collective_id=0, has_side_effects=True, vmem_limit_bytes=58 << 20),
    )(rhs[:, 0], diag_inv[:, 0], panel[:, 0], owner.reshape(3, 1, 14), target_block, jnp.transpose(row_map, (0, 2, 1, 3)))
    return got[:, None]


def solution(mesh):
    return jax.shard_map(
        shards,
        mesh=mesh,
        in_specs=(
            P(None, "prow", "pcol", None),
            P(None, "prow", "pcol", None),
            P(None, "prow", "pcol", None),
            P(None, "prow", "pcol", None),
            P(None, "prow", "pcol"),
            P(None, "prow", "pcol", None),
        ),
        out_specs=P(None, "prow", "pcol", None),
        check_vma=False,
    )
```
